256 devices in a mesh: section: 16 (over y_hi, z), rep: 16 (over x, y_lo, core).
Axes of the slice: x: 4, y: 4 (y_hi: 2, y_lo: 2; y = y_hi * 2 + y_lo), z: 8, core: 2. Of those that a mesh axis runs over, the one named last changes fastest.
Arguments:
- features: bfloat16 [32768, 256], P(('section', 'rep')), may hold values from -6 to 6
- tiles: bfloat16 [256, 64, 128, 128], P(('section', 'rep')), may hold values from 0 to 0.019042969
- columns: int32 [256, 64], P(('section', 'rep')), may hold values from 0 to 255
- weight: bfloat16 [256, 256], replicated, may hold values from -0.375 to 0.375
Outputs:
- hidden: bfloat16 [32768, 256], P(('section', 'rep'))
The draws below stay inside these ranges and needn't reach their ends.
All inputs are finite; a program needn't handle non-finite values.
Results may differ from the reference program's by a relative error of at most 0.0049.
Values may be sent and summed in bfloat16 or wider, within the bound.
No kernel may reach another device: no remote copies, remote signals or barrier semaphores. Data moves between devices by JAX's collectives and lax.ppermute only.
A program may use at most 64 MiB of HBM per device.

```python
import math
import jax
import jax.numpy as jnp
import numpy as np
from jax import lax

F = 256
BLK = 128
K = 64
NODES = 32768
NB = 256


def plant(array, stream_key, smallest, largest):
    spot = [jax.random.randint(jax.random.fold_in(stream_key, axis), (), 0, length) for axis, length in enumerate(array.shape)]
    longest = array.shape.index(max(array.shape))
    beside = spot[:longest] + [(spot[longest] + 1) % array.shape[longest]] + spot[longest + 1:]
    return array.at[tuple(spot)].set(smallest).at[tuple(beside)].set(largest)


def shard_levels(key, extent, shards, least, largest):
    def one(dim, parts):
        draws = jax.random.uniform(jax.random.fold_in(jax.random.fold_in(key, 6), dim), (parts,), jnp.float32, least / len(shards), largest / len(shards))
        return jnp.repeat(jnp.exp(draws), extent[dim] // parts).reshape((-1,) + (1,) * (len(extent) - dim - 1))

    level = one(*shards[0])
    for cut in shards[1:]:
        level = level * one(*cut)
    return level


def rank_table(number_of, skew):
    portions = [(1 << 20) // math.isqrt(rank ** skew) + 1 for rank in range(1, number_of + 1)]
    scale = 1 + sum(portions) // (1 << 30)
    return np.cumsum(np.array([max(1, weight // scale) for weight in portions]))


def ranked_ids(rng, dims, amount, slope):
    table = rank_table(amount, slope)
    lot = jax.random.randint(jax.random.fold_in(rng, 1), dims, 0, int(table[amount - 1]))
    rank = jnp.searchsorted(jnp.asarray(table, jnp.int32), lot, side="right")
    return jax.random.permutation(jax.random.fold_in(rng, 2), amount)[rank].astype(jnp.int32)


def normal_values(key, dims, scale, bound, pieces=(), kind=jnp.bfloat16):
    loudness = shard_levels(key, dims, pieces, -0.22, 0.18) if pieces else 1.0
    entries = jax.random.normal(key, dims, jnp.float32) * scale * loudness
    return jnp.minimum(jnp.maximum(entries, -bound), bound).astype(kind)


def setup_inputs(seed: int = 0) -> dict:
    streams_of = jax.random.split(jax.random.key(seed), 5)
    return {
        "features": normal_values(streams_of[0], (NODES, F), 1.0, 6.0, ((0, 256),)),
        "tiles": jnp.clip(0.019042969 * jax.random.uniform(streams_of[1], (NB, K, BLK, BLK), jnp.float32) ** shard_levels(streams_of[1], (NB, K, BLK, BLK), ((0, 256),), -0.2, 0.2), 0.0, 0.019042969).astype(jnp.bfloat16),
        "columns": plant(ranked_ids(streams_of[2], (NB, K), NB, 1), jax.random.fold_in(streams_of[2], 3), 0, NB - 1).astype(jnp.int32),
        "weight": normal_values(streams_of[3], (F, F), F ** -0.5, 0.375),
    }


def reference(features, tiles, columns, weight):
    blocks = features.reshape(NB, BLK, F)

    def one_block(pair):
        tile_rows, cols = pair
        picked = blocks[cols]
        summed = jnp.einsum("kij,kjf->if", tile_rows.astype(jnp.float32), picked.astype(jnp.float32))
        return summed.astype(jnp.bfloat16)

    aggregated = lax.map(one_block, (tiles, columns)).reshape(NODES, F)
    product = jnp.dot(aggregated, weight, preferred_element_type=jnp.float32)
    return jnp.maximum(product, 0.0).astype(jnp.bfloat16)
```

```python
import itertools

import jax
import jax.numpy as jnp
from jax import lax
from jax.experimental import pallas as pl
from jax.experimental.pallas import tpu as pltpu
from jax.sharding import Mesh, PartitionSpec as P

AXES = ("yh", "z", "x", "yl", "core")
DIMS = (2, 8, 4, 2, 2)
SIDE = 128
WIDTH = 256
TILES = 64
HALF = 16
BATCH = 4


def pairs(target):
    found = []
    for source, (yh, z, x, yl, core) in enumerate(itertools.product(*map(range, DIMS))):
        tx, ty, tz, tc = target(x, yh * 2 + yl, z, core)
        tx, ty, tz = tx % 4, ty % 4, tz % 8
        found.append((source, ((((ty // 2) * 8 + tz) * 4 + tx) * 2 + ty % 2) * 2 + tc))
    return found


def from_z(a, d):
    return lax.ppermute(a, AXES, pairs(lambda x, y, z, c: (x, y, z - d, c)))


def from_middle(a, d):
    return lax.ppermute(a, AXES, pairs(lambda x, y, z, c: (x, y - d, z, c) if c == 0 else (x - d, y, z, c)))


def from_last(a, d):
    return lax.ppermute(a, AXES, pairs(lambda x, y, z, c: (x - d, y, z, c) if c == 0 else (x, y - d, z, c)))


def from_core(a):
    return lax.ppermute(a, "core", [(0, 1), (1, 0)])


def places(columns):
    yh, z, x, yl, core = (lax.axis_index(a) for a in AXES)
    y = yh * 2 + yl
    dz = (((columns >> 4) & 7) - z) & 7
    dx = (((columns >> 2) & 3) - x) & 3
    dy = (((columns >> 7) * 2 + ((columns >> 1) & 1)) - y) & 3
    middle = jnp.where(core == 0, dy, dx)
    last = jnp.where(core == 0, dx, dy)
    return jnp.where((columns & 1) == core, last * 32 + middle * 8 + dz, -1)


def multiply_kernel(place_ref, tiles_ref, *rest):
    pieces, (out_ref, list_ref, count_ref) = rest[:-3], rest[-3:]
    for p in range(8):
        count_ref[p] = 0

    @pl.loop(0, TILES)
    def _(k):
        place = place_ref[0, k]

        @pl.when(place >= 0)
        def _():
            piece = place // HALF
            n = count_ref[piece]
            list_ref[piece, n] = k * HALF + place % HALF
            count_ref[piece] = n + 1

    out_ref[...] = jnp.zeros_like(out_ref)
    for p in range(8):
        ref = pieces[max(p - 1, 0)]
        base = HALF if p == 1 else 0
        n = count_ref[p]

        @pl.loop(0, (n + BATCH - 1) // BATCH)
        def _(i):
            left, right = [], []
            for j in range(BATCH):
                at = i * BATCH + j
                code = list_ref[p, jnp.minimum(at, n - 1)]
                tile = tiles_ref[pl.ds(pl.multiple_of((code // HALF) * SIDE, SIDE), SIDE), :]
                left.append(jnp.where(at < n, tile, jnp.zeros_like(tile)))
                right.append(ref[pl.ds(pl.multiple_of((base + code % HALF) * SIDE, SIDE), SIDE), :])
            out_ref[...] += jnp.dot(
                jnp.concatenate(left, axis=1), jnp.concatenate(right, axis=0), preferred_element_type=jnp.float32
            )


def multiply(place, tiles, pieces):
    vmem = pl.BlockSpec(memory_space=pltpu.VMEM)
    return pl.pallas_call(
        multiply_kernel,
        out_shape=jax.ShapeDtypeStruct((SIDE, WIDTH), jnp.float32),
        in_specs=[pl.BlockSpec(memory_space=pltpu.SMEM), vmem] + [vmem] * len(pieces),
        out_specs=vmem,
        scratch_shapes=[pltpu.SMEM((8, TILES), jnp.int32), pltpu.SMEM((8,), jnp.int32)],
        compiler_params=pltpu.CompilerParams(vmem_limit_bytes=24 * 1024 * 1024),
        cost_estimate=pl.CostEstimate(flops=32 * 2 * SIDE * SIDE * WIDTH, bytes_accessed=10 << 20, transcendentals=0),
    )(place, tiles, *pieces)


def gather(own):
    p1, m1, p2, m2 = (from_z(own, d) for d in (1, -1, 2, -2))
    p3, m3, p4 = from_z(p2, 1), from_z(m2, -1), from_z(p2, 2)
    line = jnp.concatenate([own, p1, p2, p3, p4, m3, m2, m1], axis=0)
    plane = jnp.concatenate([line] + [from_middle(line, d) for d in (1, 2, 3)], axis=0)
    half = HALF * SIDE
    low, high = plane[:half], plane[half:]
    next_low, prev_high = from_last(low, 1), from_last(high, -1)
    next_high, prev_low = from_last(high, 1), from_last(low, -1)
    far_low, far_high = from_last(next_low, 1), from_last(prev_high, -1)
    return [plane, next_low, next_high, far_low, far_high, prev_low, prev_high]


def on_device(features, tiles, columns, weight):
    mine = tiles.reshape(TILES * SIDE, SIDE)
    other = from_core(mine)
    pieces = gather(features)
    away = multiply(places(from_core(columns)), other, pieces)
    back = from_core(away)
    here = multiply(places(columns), mine, pieces)
    aggregated = (here + back).astype(jnp.bfloat16)
    product = jnp.dot(aggregated, weight, preferred_element_type=jnp.float32)
    return jnp.maximum(product, 0.0).astype(jnp.bfloat16)


def solution(mesh):
    grid = Mesh(mesh.devices.reshape(DIMS), AXES)
    return jax.shard_map(
        on_device,
        mesh=grid,
        in_specs=(P(AXES, None), P(AXES, None, None, None), P(AXES, None), P()),
        out_specs=P(AXES, None),
        check_vma=False,
    )
```

```python
import itertools

import jax
import jax.numpy as jnp
from jax import lax
from jax.experimental import pallas as pl
from jax.experimental.pallas import tpu as pltpu
from jax.sharding import Mesh, PartitionSpec as P

AXES = ("yh", "zh", "zl", "x", "yl", "core")
DIMS = (2, 4, 2, 4, 2, 2)
SIDE = 128
WIDTH = 256
TILES = 64
PLANE = 16
BUFFERS = 8
AHEAD = 14
BATCH = 16


def move(a, target):
    found = []
    for source, (yh, zh, zl, x, yl, core) in enumerate(itertools.product(*map(range, DIMS))):
        tx, ty, tz, tc = target(x, yh * 2 + yl, zh * 2 + zl, core)
        tx, ty, tz = tx % 4, ty % 4, tz % 8
        found.append((source, ((((ty // 2) * 8 + tz) * 4 + tx) * 2 + ty % 2) * 2 + tc))
    return lax.ppermute(a, AXES, found)


def from_line(a, d):
    return move(a, lambda x, y, z, c: (x, y, z - 2 * d, c))


def from_middle(a, d):
    return move(a, lambda x, y, z, c: (x, y - d, z, c) if c == 0 else (x - d, y, z, c))


def from_last(a, d):
    return move(a, lambda x, y, z, c: (x - d, y, z, c) if c == 0 else (x, y - d, z, c))


def from_core(a):
    return move(a, lambda x, y, z, c: (x, y, z, 1 - c))


def from_pair(a):
    return move(a, lambda x, y, z, c: (x, y, z ^ 1, c))


def places(columns):
    yh, zh, zl, x, yl, core = (lax.axis_index(a) for a in AXES)
    y = yh * 2 + yl
    at = columns & 1
    dz = (((columns >> 5) & 3) - zh) & 3
    dx = (((columns >> 2) & 3) - x) & 3
    dy = (((columns >> 7) * 2 + ((columns >> 1) & 1)) - y) & 3
    middle = jnp.where(at == 0, dy, dx)
    last = jnp.where(at == 0, dx, dy)
    place = ((at ^ core) * 4 + last) * PLANE + middle * 4 + dz
    return jnp.where(((columns >> 4) & 1) == zl, place, -1)


def list_kernel(place_ref, list_ref):
    for r in range(2):

        def step(k, n):
            place = place_ref[r, k]
            list_ref[r, n] = (k << 7) + (place & 127)
            return jnp.where(place >= 0, n + 1, n)

        list_ref[r, TILES] = lax.fori_loop(0, TILES, step, 0)


def listed(place):
    smem = pl.BlockSpec(memory_space=pltpu.SMEM)
    return pl.pallas_call(
        list_kernel,
        out_shape=jax.ShapeDtypeStruct((2, TILES + 1), jnp.int32),
        in_specs=[smem],
        out_specs=smem,
        compiler_params=pltpu.CompilerParams(vmem_limit_bytes=1024 * 1024),
    )(place)


def rows(index):
    return pl.ds(pl.multiple_of(index << 7, SIDE), SIDE)


def multiply(row, lists, parts, buffers):
    vmem = pl.BlockSpec(memory_space=pltpu.VMEM)
    smem = pl.BlockSpec(memory_space=pltpu.SMEM)
    split = AHEAD

    def kernel(list_ref, *rest):
        part_refs, held, out_ref = rest[: len(parts)], rest[len(parts) : -1], rest[-1]
        out_ref[...] = jnp.zeros_like(out_ref)
        n = list_ref[row, TILES]

        @pl.loop(0, (n + BATCH - 1) // BATCH)
        def _(i):
            left, right = [], []
            for j in range(BATCH):
                at = i * BATCH + j
                code = list_ref[row, jnp.minimum(at, n - 1)]
                k = code >> 7
                if len(parts) == 1:
                    tile = part_refs[0][rows(k), :]
                else:
                    tile = part_refs[0][rows(jnp.minimum(k, split - 1)), :]
                    tile = jnp.where(k < split, tile, part_refs[1][rows(jnp.maximum(k - split, 0)), :])
                left.append(jnp.where(at < n, tile, jnp.zeros_like(tile)))
                here = rows(code & 15)
                buffer = (code >> 4) & 7
                block = held[0][here, :]
                for b in range(1, BUFFERS):
                    block = jnp.where(buffer == b, held[b][here, :], block)
                right.append(block)
            out_ref[...] += jnp.dot(
                jnp.concatenate(left, axis=1), jnp.concatenate(right, axis=0), preferred_element_type=jnp.float32
            )

    held = [pltpu.with_memory_space_constraint(a, pltpu.VMEM) for a in (*parts, *buffers)]
    return pl.pallas_call(
        kernel,
        out_shape=jax.ShapeDtypeStruct((SIDE, WIDTH), jnp.float32),
        in_specs=[smem] + [vmem] * len(held),
        out_specs=vmem,
        compiler_params=pltpu.CompilerParams(vmem_limit_bytes=16 * 1024 * 1024),
        cost_estimate=pl.CostEstimate(flops=32 * 2 * SIDE * SIDE * WIDTH, bytes_accessed=3 << 20, transcendentals=0),
    )(lists, *held)


def together(*arrays):
    return lax.optimization_barrier(arrays)


def on_device(features, tiles, columns, weight):
    mine = tiles.reshape(TILES * SIDE, SIDE)
    place = places(jnp.concatenate([columns, from_pair(columns)], axis=0))
    line = jnp.concatenate([features] + [from_line(features, d) for d in (1, 2, 3)], axis=0)
    line, place, ahead = together(line, place, mine[: AHEAD * SIDE])
    first = from_pair(ahead)
    plane = jnp.concatenate([line] + [from_middle(line, d) for d in (1, 2, 3)], axis=0)
    plane, lists, first, behind = together(plane, listed(place), first, mine[AHEAD * SIDE :])
    rest = from_pair(behind)
    buffers = [plane] + [from_last(plane, d) for d in (1, 2, 3)]
    buffers += [from_core(a) for a in buffers]
    across = from_pair(multiply(1, lists, [first, rest], buffers))
    here = multiply(0, lists, [mine], buffers)
    aggregated = (here + across).astype(jnp.bfloat16)
    product = jnp.dot(aggregated, weight, preferred_element_type=jnp.float32)
    return jnp.maximum(product, 0.0).astype(jnp.bfloat16)


def solution(mesh):
    grid = Mesh(mesh.devices.reshape(DIMS), AXES)
    return jax.shard_map(
        on_device,
        mesh=grid,
        in_specs=(P(AXES, None), P(AXES, None, None, None), P(AXES, None), P()),
        out_specs=P(AXES, None),
        check_vma=False,
    )
```

```python
import itertools

import jax
import jax.numpy as jnp
from jax import lax
from jax.experimental import pallas as pl
from jax.experimental.pallas import tpu as pltpu
from jax.sharding import Mesh, PartitionSpec as P

AXES = ("yh", "zh", "zl", "x", "yl", "core")
DIMS = (2, 4, 2, 4, 2, 2)
SIDE = 128
WIDTH = 256
TILES = 64
PLANE = 16
BUFFERS = 8
AHEAD = 14
BATCH = 16


def move(a, target):
    found = []
    for source, (yh, zh, zl, x, yl, core) in enumerate(itertools.product(*map(range, DIMS))):
        tx, ty, tz, tc = target(x, yh * 2 + yl, zh * 2 + zl, core)
        tx, ty, tz = tx % 4, ty % 4, tz % 8
        found.append((source, ((((ty // 2) * 8 + tz) * 4 + tx) * 2 + ty % 2) * 2 + tc))
    return lax.ppermute(a, AXES, found)


def from_line(a, d):
    return move(a, lambda x, y, z, c: (x, y, z - 2 * d, c))


def from_middle(a, d):
    return move(a, lambda x, y, z, c: (x, y - d, z, c) if c == 0 else (x - d, y, z, c))


def from_last(a, d):
    return move(a, lambda x, y, z, c: (x - d, y, z, c) if c == 0 else (x, y - d, z, c))


def from_core(a):
    return move(a, lambda x, y, z, c: (x, y, z, 1 - c))


def from_pair(a):
    return move(a, lambda x, y, z, c: (x, y, z ^ 1, c))


def places(columns):
    yh, zh, zl, x, yl, core = (lax.axis_index(a) for a in AXES)
    y = yh * 2 + yl
    at = columns & 1
    dz = (((columns >> 5) & 3) - zh) & 3
    dx = (((columns >> 2) & 3) - x) & 3
    dy = (((columns >> 7) * 2 + ((columns >> 1) & 1)) - y) & 3
    middle = jnp.where(at == 0, dy, dx)
    last = jnp.where(at == 0, dx, dy)
    place = ((at ^ core) * 4 + last) * PLANE + middle * 4 + dz
    return jnp.where(((columns >> 4) & 1) == zl, place, -1)


def list_kernel(place_ref, list_ref):
    for r in range(2):

        def step(k, n):
            place = place_ref[r, k]
            list_ref[r, n] = (k << 7) + (place & 127)
            return jnp.where(place >= 0, n + 1, n)

        list_ref[r, TILES] = lax.fori_loop(0, TILES, step, 0)


def listed(place):
    smem = pl.BlockSpec(memory_space=pltpu.SMEM)
    return pl.pallas_call(
        list_kernel,
        out_shape=jax.ShapeDtypeStruct((2, TILES + 1), jnp.int32),
        in_specs=[smem],
        out_specs=smem,
        compiler_params=pltpu.CompilerParams(vmem_limit_bytes=1024 * 1024),
    )(place)


def rows(index):
    return pl.ds(pl.multiple_of(index << 7, SIDE), SIDE)


def multiply(row, lists, parts, buffers):
    vmem = pl.BlockSpec(memory_space=pltpu.VMEM)
    smem = pl.BlockSpec(memory_space=pltpu.SMEM)
    split = AHEAD

    def kernel(list_ref, *rest):
        part_refs, held, out_ref = rest[: len(parts)], rest[len(parts) : -1], rest[-1]
        out_ref[...] = jnp.zeros_like(out_ref)
        n = list_ref[row, TILES]

        @pl.loop(0, (n + BATCH - 1) // BATCH)
        def _(i):
            left, right = [], []
            for j in range(BATCH):
                at = i * BATCH + j
                code = list_ref[row, jnp.minimum(at, n - 1)]
                k = code >> 7
                if len(parts) == 1:
                    tile = part_refs[0][rows(k), :]
                else:
                    tile = part_refs[0][rows(jnp.minimum(k, split - 1)), :]
                    tile = jnp.where(k < split, tile, part_refs[1][rows(jnp.maximum(k - split, 0)), :])
                left.append(jnp.where(at < n, tile, jnp.zeros_like(tile)))
                here = rows(code & 15)
                buffer = (code >> 4) & 7
                block = held[0][here, :]
                for b in range(1, BUFFERS):
                    block = jnp.where(buffer == b, held[b][here, :], block)
                right.append(block)
            out_ref[...] += jnp.dot(
                jnp.concatenate(left, axis=1), jnp.concatenate(right, axis=0), preferred_element_type=jnp.float32
            )

    held = [pltpu.with_memory_space_constraint(a, pltpu.VMEM) for a in (*parts, *buffers)]
    return pl.pallas_call(
        kernel,
        out_shape=jax.ShapeDtypeStruct((SIDE, WIDTH), jnp.float32),
        in_specs=[smem] + [vmem] * len(held),
        out_specs=vmem,
        compiler_params=pltpu.CompilerParams(vmem_limit_bytes=16 * 1024 * 1024),
        cost_estimate=pl.CostEstimate(flops=32 * 2 * SIDE * SIDE * WIDTH, bytes_accessed=3 << 20, transcendentals=0),
    )(lists, *held)


def together(*arrays):
    return lax.optimization_barrier(arrays)


def on_device(features, tiles, columns, weight):
    mine = tiles.reshape(TILES * SIDE, SIDE)
    place = places(jnp.concatenate([columns, from_pair(columns)], axis=0))
    lines = [features] + [from_line(features, d) for d in (1, 2, 3)]
    lines[1], sent = together(lines[1], mine)
    line = jnp.concatenate(lines, axis=0)
    line, place = together(line, place)
    paired = from_pair(sent)
    plane = jnp.concatenate([line] + [from_middle(line, d) for d in (1, 2, 3)], axis=0)
    plane, place = together(plane, place)
    lists = listed(place)
    buffers = [plane] + [from_last(plane, d) for d in (1, 2, 3)]
    buffers += [from_core(a) for a in buffers]
    paired = together(paired)[0]
    across = from_pair(multiply(1, lists, [paired], buffers))
    here = multiply(0, lists, [mine], buffers)
    aggregated = (here + across).astype(jnp.bfloat16)
    product = jnp.dot(aggregated, weight, preferred_element_type=jnp.float32)
    return jnp.maximum(product, 0.0).astype(jnp.bfloat16)


def solution(mesh):
    grid = Mesh(mesh.devices.reshape(DIMS), AXES)
    return jax.shard_map(
        on_device,
        mesh=grid,
        in_specs=(P(AXES, None), P(AXES, None, None, None), P(AXES, None), P()),
        out_specs=P(AXES, None),
        check_vma=False,
    )
```

```python
import itertools

import jax
import jax.numpy as jnp
from jax import lax
from jax.experimental import pallas as pl
from jax.experimental.pallas import tpu as pltpu
from jax.sharding import Mesh, PartitionSpec as P

AXES = ("yh", "zh", "zl", "x", "yl", "core")
DIMS = (2, 4, 2, 4, 2, 2)
SIDE = 128
WIDTH = 256
TILES = 64
PLANE = 16
BATCH = 16


def move(a, target):
    found = []
    for source, (yh, zh, zl, x, yl, core) in enumerate(itertools.product(*map(range, DIMS))):
        tx, ty, tz, tc = target(x, yh * 2 + yl, zh * 2 + zl, core)
        tx, ty, tz = tx % 4, ty % 4, tz % 8
        found.append((source, ((((ty // 2) * 8 + tz) * 4 + tx) * 2 + ty % 2) * 2 + tc))
    return lax.ppermute(a, AXES, found)


def from_line(a, d):
    return move(a, lambda x, y, z, c: (x, y, z - 2 * d, c))


def from_middle(a, d):
    return move(a, lambda x, y, z, c: (x, y - d, z, c) if c == 0 else (x - d, y, z, c))


def from_last(a, d):
    return move(a, lambda x, y, z, c: (x - d, y, z, c) if c == 0 else (x, y - d, z, c))


def from_core(a):
    return move(a, lambda x, y, z, c: (x, y, z, 1 - c))


def from_lender(a):
    return move(a, lambda x, y, z, c: (x, y, z + 1 - 2 * c, c))


def from_borrower(a):
    return move(a, lambda x, y, z, c: (x, y, z - 1 + 2 * c, c))


def places(columns):
    yh, zh, zl, x, yl, core = (lax.axis_index(a) for a in AXES)
    y = yh * 2 + yl
    at = columns & 1
    dz = (((columns >> 5) & 3) - zh) & 3
    dx = (((columns >> 2) & 3) - x) & 3
    dy = (((columns >> 7) * 2 + ((columns >> 1) & 1)) - y) & 3
    middle = jnp.where(at == 0, dy, dx)
    last = jnp.where(at == 0, dx, dy)
    inner = middle * 4 + dz
    buffer = jnp.where(last == 0, 0, last * 2 - 1 + (inner >> 3))
    place = ((at ^ core) * 7 + buffer) * PLANE + inner
    return jnp.where(((columns >> 4) & 1) == zl, place, -1)


def list_kernel(place_ref, list_ref):
    for r in range(2):

        def step(k, n):
            place = place_ref[r, k]
            list_ref[r, n] = (k << 8) + (place & 255)
            return jnp.where(place >= 0, n + 1, n)

        list_ref[r, TILES] = lax.fori_loop(0, TILES, step, 0)


def listed(place):
    smem = pl.BlockSpec(memory_space=pltpu.SMEM)
    return pl.pallas_call(
        list_kernel,
        out_shape=jax.ShapeDtypeStruct((2, TILES + 1), jnp.int32),
        in_specs=[smem],
        out_specs=smem,
        compiler_params=pltpu.CompilerParams(vmem_limit_bytes=1024 * 1024),
    )(place)


def rows(index):
    return pl.ds(pl.multiple_of(index << 7, SIDE), SIDE)


def multiply(row, lists, tiles, buffers):
    vmem = pl.BlockSpec(memory_space=pltpu.VMEM)

    def kernel(list_ref, tiles_ref, *rest):
        held, out_ref = rest[:-1], rest[-1]
        out_ref[...] = jnp.zeros_like(out_ref)
        n = list_ref[row, TILES]

        @pl.loop(0, (n + BATCH - 1) // BATCH)
        def _(i):
            left, right = [], []
            for j in range(BATCH):
                at = i * BATCH + j
                code = list_ref[row, jnp.minimum(at, n - 1)]
                tile = tiles_ref[rows(code >> 8), :]
                left.append(jnp.where(at < n, tile, jnp.zeros_like(tile)))
                here = rows(code & 15)
                buffer = (code >> 4) & 15
                block = None
                for b, ref in enumerate(held):
                    within = here if ref.shape[0] == PLANE * SIDE else rows(code & 7)
                    found = ref[within, :]
                    block = found if block is None else jnp.where(buffer == b, found, block)
                right.append(block)
            out_ref[...] += jnp.dot(
                jnp.concatenate(left, axis=1), jnp.concatenate(right, axis=0), preferred_element_type=jnp.float32
            )

    held = [pltpu.with_memory_space_constraint(a, pltpu.VMEM) for a in (tiles, *buffers)]
    return pl.pallas_call(
        kernel,
        out_shape=jax.ShapeDtypeStruct((SIDE, WIDTH), jnp.float32),
        in_specs=[pl.BlockSpec(memory_space=pltpu.SMEM)] + [vmem] * len(held),
        out_specs=vmem,
        compiler_params=pltpu.CompilerParams(vmem_limit_bytes=16 * 1024 * 1024),
        cost_estimate=pl.CostEstimate(flops=32 * 2 * SIDE * SIDE * WIDTH, bytes_accessed=3 << 20, transcendentals=0),
    )(lists, *held)


def together(*arrays):
    return lax.optimization_barrier(arrays)


def on_device(features, tiles, columns, weight):
    mine = tiles.reshape(TILES * SIDE, SIDE)
    place = places(jnp.concatenate([columns, from_lender(columns)], axis=0))
    lines = [features] + [from_line(features, d) for d in (1, 2, 3)]
    lines[1], sent = together(lines[1], mine)
    line = jnp.concatenate(lines, axis=0)
    line, place = together(line, place)
    lent = from_lender(sent)
    plane = jnp.concatenate([line] + [from_middle(line, d) for d in (1, 2, 3)], axis=0)
    plane, place = together(plane, place)
    lists = listed(place)
    half = PLANE // 2 * SIDE
    low, high = plane[:half], plane[half:]
    after_low, before_high = from_last(low, 1), from_last(high, -1)
    after_low, before_high, lists = together(after_low, before_high, lists)
    after_high, before_low = from_last(high, 1), from_last(low, -1)
    buffers = [plane, after_low, after_high, from_last(after_low, 1), from_last(before_high, -1), before_low, before_high]
    buffers += [from_core(a) for a in buffers]
    lent = together(lent)[0]
    back = from_borrower(multiply(1, lists, lent, buffers))
    here = multiply(0, lists, mine, buffers)
    aggregated = (here + back).astype(jnp.bfloat16)
    product = jnp.dot(aggregated, weight, preferred_element_type=jnp.float32)
    return jnp.maximum(product, 0.0).astype(jnp.bfloat16)


def solution(mesh):
    grid = Mesh(mesh.devices.reshape(DIMS), AXES)
    return jax.shard_map(
        on_device,
        mesh=grid,
        in_specs=(P(AXES, None), P(AXES, None, None, None), P(AXES, None), P()),
        out_specs=P(AXES, None),
        check_vma=False,
    )
```

```python
import itertools

import jax
import jax.numpy as jnp
from jax import lax
from jax.experimental import pallas as pl
from jax.experimental.pallas import tpu as pltpu
from jax.sharding import Mesh, PartitionSpec as P

AXES = ("yh", "zh", "zl", "x", "yl", "core")
DIMS = (2, 4, 2, 4, 2, 2)
SIDE = 128
WIDTH = 256
TILES = 64
PLANE = 16
BATCH = 16


def move(a, target):
    found = []
    for source, (yh, zh, zl, x, yl, core) in enumerate(itertools.product(*map(range, DIMS))):
        tx, ty, tz, tc = target(x, yh * 2 + yl, zh * 2 + zl, core)
        tx, ty, tz = tx % 4, ty % 4, tz % 8
        found.append((source, ((((ty // 2) * 8 + tz) * 4 + tx) * 2 + ty % 2) * 2 + tc))
    return lax.ppermute(a, AXES, found)


def from_line(a, d):
    return move(a, lambda x, y, z, c: (x, y, z - 2 * d, c))


def from_middle(a, d):
    return move(a, lambda x, y, z, c: (x, y - d, z, c) if c == 0 else (x - d, y, z, c))


def from_last(a, d):
    return move(a, lambda x, y, z, c: (x - d, y, z, c) if c == 0 else (x, y - d, z, c))


def from_core(a):
    return move(a, lambda x, y, z, c: (x, y, z, 1 - c))


def from_lender(a):
    return move(a, lambda x, y, z, c: (x, y, z + 1 - 2 * c, c))


def from_borrower(a):
    return move(a, lambda x, y, z, c: (x, y, z - 1 + 2 * c, c))


def places(columns):
    yh, zh, zl, x, yl, core = (lax.axis_index(a) for a in AXES)
    y = yh * 2 + yl
    at = columns & 1
    dz = (((columns >> 5) & 3) - zh) & 3
    dx = (((columns >> 2) & 3) - x) & 3
    dy = (((columns >> 7) * 2 + ((columns >> 1) & 1)) - y) & 3
    middle = jnp.where(at == 0, dy, dx)
    last = jnp.where(at == 0, dx, dy)
    inner = middle * 4 + dz
    buffer = jnp.where(last == 0, 0, last * 2 - 1 + (inner >> 3))
    place = ((at ^ core) * 7 + buffer) * PLANE + inner
    return jnp.where(((columns >> 4) & 1) == zl, place, -1)


def list_kernel(place_ref, list_ref):
    for r in range(2):

        def step(k, n):
            place = place_ref[r, k]
            list_ref[r, n] = (k << 8) + (place & 255)
            return jnp.where(place >= 0, n + 1, n)

        list_ref[r, TILES] = lax.fori_loop(0, TILES, step, 0)


def listed(place):
    smem = pl.BlockSpec(memory_space=pltpu.SMEM)
    return pl.pallas_call(
        list_kernel,
        out_shape=jax.ShapeDtypeStruct((2, TILES + 1), jnp.int32),
        in_specs=[smem],
        out_specs=smem,
        compiler_params=pltpu.CompilerParams(vmem_limit_bytes=1024 * 1024),
    )(place)


def rows(index):
    return pl.ds(pl.multiple_of(index << 7, SIDE), SIDE)


def multiply(row, lists, tiles, buffers):
    vmem = pl.BlockSpec(memory_space=pltpu.VMEM)

    def kernel(list_ref, tiles_ref, *rest):
        held, out_ref = rest[:-1], rest[-1]
        out_ref[...] = jnp.zeros_like(out_ref)
        n = list_ref[row, TILES]

        @pl.loop(0, (n + BATCH - 1) // BATCH)
        def _(i):
            left, right = [], []
            for j in range(BATCH):
                at = i * BATCH + j
                code = list_ref[row, jnp.minimum(at, n - 1)]
                tile = tiles_ref[rows(code >> 8), :]
                left.append(jnp.where(at < n, tile, jnp.zeros_like(tile)))
                here = rows(code & 15)
                buffer = (code >> 4) & 15
                block = None
                for b, ref in enumerate(held):
                    within = here if ref.shape[0] == PLANE * SIDE else rows(code & 7)
                    found = ref[within, :]
                    block = found if block is None else jnp.where(buffer == b, found, block)
                right.append(block)
            out_ref[...] += jnp.dot(
                jnp.concatenate(left, axis=1), jnp.concatenate(right, axis=0), preferred_element_type=jnp.float32
            )

    held = [pltpu.with_memory_space_constraint(a, pltpu.VMEM) for a in (tiles, *buffers)]
    return pl.pallas_call(
        kernel,
        out_shape=jax.ShapeDtypeStruct((SIDE, WIDTH), jnp.float32),
        in_specs=[pl.BlockSpec(memory_space=pltpu.SMEM)] + [vmem] * len(held),
        out_specs=vmem,
        compiler_params=pltpu.CompilerParams(vmem_limit_bytes=16 * 1024 * 1024),
        cost_estimate=pl.CostEstimate(flops=32 * 2 * SIDE * SIDE * WIDTH, bytes_accessed=3 << 20, transcendentals=0),
    )(lists, *held)


def together(*arrays):
    return lax.optimization_barrier(arrays)


def on_device(features, tiles, columns, weight):
    mine = tiles.reshape(TILES * SIDE, SIDE)
    place = places(jnp.concatenate([columns, from_lender(columns)], axis=0))
    lines = [features] + [from_line(features, d) for d in (1, 2, 3)]
    line = jnp.concatenate(lines, axis=0)
    line, place, sent = together(line, place, mine)
    lent = from_lender(sent)
    plane = jnp.concatenate([line] + [from_middle(line, d) for d in (1, 2, 3)], axis=0)
    plane, place = together(plane, place)
    lists = listed(place)
    half = PLANE // 2 * SIDE
    low, high = plane[:half], plane[half:]
    after_low, before_high = from_last(low, 1), from_last(high, -1)
    after_low, before_high, lists = together(after_low, before_high, lists)
    after_high, before_low = from_last(high, 1), from_last(low, -1)
    after_high, before_low, lent = together(after_high, before_low, lent)
    buffers = [plane, after_low, after_high, from_last(after_low, 1), from_last(before_high, -1), before_low, before_high]
    buffers += [from_core(a) for a in buffers]
    back = from_borrower(multiply(1, lists, lent, buffers))
    here = multiply(0, lists, mine, buffers)
    aggregated = (here + back).astype(jnp.bfloat16)
    product = jnp.dot(aggregated, weight, preferred_element_type=jnp.float32)
    return jnp.maximum(product, 0.0).astype(jnp.bfloat16)


def solution(mesh):
    grid = Mesh(mesh.devices.reshape(DIMS), AXES)
    return jax.shard_map(
        on_device,
        mesh=grid,
        in_specs=(P(AXES, None), P(AXES, None, None, None), P(AXES, None), P()),
        out_specs=P(AXES, None),
        check_vma=False,
    )
```

```python
import itertools

import jax
import jax.numpy as jnp
from jax import lax
from jax.experimental import pallas as pl
from jax.experimental.pallas import tpu as pltpu
from jax.sharding import Mesh, PartitionSpec as P

AXES = ("yh", "zh", "zl", "x", "yl", "core")
DIMS = (2, 4, 2, 4, 2, 2)
SIDE = 128
WIDTH = 256
TILES = 64
PLANE = 16
BUFFERS = 7
BATCH = 8


def move(a, target):
    found = []
    for source, (yh, zh, zl, x, yl, core) in enumerate(itertools.product(*map(range, DIMS))):
        tx, ty, tz, tc = target(x, yh * 2 + yl, zh * 2 + zl, core)
        tx, ty, tz = tx % 4, ty % 4, tz % 8
        found.append((source, ((((ty // 2) * 8 + tz) * 4 + tx) * 2 + ty % 2) * 2 + tc))
    return lax.ppermute(a, AXES, found)


def from_line(a, d):
    return move(a, lambda x, y, z, c: (x, y, z - 2 * d, c))


def from_middle(a, d):
    return move(a, lambda x, y, z, c: (x, y - d, z, c) if c == 0 else (x - d, y, z, c))


def from_last(a, d):
    return move(a, lambda x, y, z, c: (x - d, y, z, c) if c == 0 else (x, y - d, z, c))


def from_core(a):
    return move(a, lambda x, y, z, c: (x, y, z, 1 - c))


def from_lender(a):
    return move(a, lambda x, y, z, c: (x, y, z + 1 - 2 * c, c))


def from_borrower(a):
    return move(a, lambda x, y, z, c: (x, y, z - 1 + 2 * c, c))


def places(columns):
    yh, zh, zl, x, yl, core = (lax.axis_index(a) for a in AXES)
    y = yh * 2 + yl
    at = columns & 1
    dz = (((columns >> 5) & 3) - zh) & 3
    dx = (((columns >> 2) & 3) - x) & 3
    dy = (((columns >> 7) * 2 + ((columns >> 1) & 1)) - y) & 3
    middle = jnp.where(at == 0, dy, dx)
    last = jnp.where(at == 0, dx, dy)
    inner = middle * 4 + dz
    buffer = jnp.where(last == 0, 0, last * 2 - 1 + (inner >> 3))
    place = ((at ^ core) * BUFFERS + buffer) * PLANE + inner
    return jnp.where(((columns >> 4) & 1) == zl, place, -1)


def list_kernel(place_ref, list_ref):
    for r in range(2):

        def step(k, counts):
            place = place_ref[r, k]
            held, far = place >= 0, place >= BUFFERS * PLANE
            list_ref[2 * r, counts[0]] = (k << 8) + (place & 255)
            list_ref[2 * r + 1, counts[1]] = (k << 8) + ((place - BUFFERS * PLANE) & 255)
            return jnp.where(held & ~far, counts[0] + 1, counts[0]), jnp.where(far, counts[1] + 1, counts[1])

        counts = lax.fori_loop(0, TILES, step, (0, 0))
        list_ref[2 * r, TILES] = counts[0]
        list_ref[2 * r + 1, TILES] = counts[1]


def listed(place):
    smem = pl.BlockSpec(memory_space=pltpu.SMEM)
    return pl.pallas_call(
        list_kernel,
        out_shape=jax.ShapeDtypeStruct((4, TILES + 1), jnp.int32),
        in_specs=[smem],
        out_specs=smem,
        compiler_params=pltpu.CompilerParams(vmem_limit_bytes=1024 * 1024),
    )(place)


def rows(index):
    return pl.ds(pl.multiple_of(index << 7, SIDE), SIDE)


def multiply(row, lists, tiles, buffers):
    vmem = pl.BlockSpec(memory_space=pltpu.VMEM)

    def kernel(list_ref, tiles_ref, *rest):
        out_ref = rest[-1]
        out_ref[...] = jnp.zeros_like(out_ref)
        for side in range(2):
            held = rest[side * BUFFERS : (side + 1) * BUFFERS]
            which = 2 * row + side
            n = list_ref[which, TILES]

            @pl.loop(0, (n + BATCH - 1) // BATCH)
            def _(i):
                left, right = [], []
                for j in range(BATCH):
                    at = i * BATCH + j
                    code = list_ref[which, jnp.minimum(at, n - 1)]
                    tile = tiles_ref[rows(code >> 8), :]
                    left.append(jnp.where(at < n, tile, jnp.zeros_like(tile)))
                    buffer = (code >> 4) & 15
                    block = held[0][rows(code & 15), :]
                    for b in range(1, BUFFERS):
                        block = jnp.where(buffer == b, held[b][rows(code & 7), :], block)
                    right.append(block)
                out_ref[...] += jnp.dot(
                    jnp.concatenate(left, axis=1), jnp.concatenate(right, axis=0), preferred_element_type=jnp.float32
                )

    held = [pltpu.with_memory_space_constraint(a, pltpu.VMEM) for a in (tiles, *buffers)]
    return pl.pallas_call(
        kernel,
        out_shape=jax.ShapeDtypeStruct((SIDE, WIDTH), jnp.float32),
        in_specs=[pl.BlockSpec(memory_space=pltpu.SMEM)] + [vmem] * len(held),
        out_specs=vmem,
        compiler_params=pltpu.CompilerParams(vmem_limit_bytes=16 * 1024 * 1024),
        cost_estimate=pl.CostEstimate(flops=32 * 2 * SIDE * SIDE * WIDTH, bytes_accessed=3 << 20, transcendentals=0),
    )(lists, *held)


def together(*arrays):
    return lax.optimization_barrier(arrays)


def on_device(features, tiles, columns, weight):
    mine = tiles.reshape(TILES * SIDE, SIDE)
    place = places(jnp.concatenate([columns, from_lender(columns)], axis=0))
    lines = [features] + [from_line(features, d) for d in (1, 2, 3)]
    line = jnp.concatenate(lines, axis=0)
    line, place, sent = together(line, place, mine)
    lent = from_lender(sent)
    plane = jnp.concatenate([line] + [from_middle(line, d) for d in (1, 2, 3)], axis=0)
    plane, place = together(plane, place)
    lists = listed(place)
    half = PLANE // 2 * SIDE
    low, high = plane[:half], plane[half:]
    after_low, before_high = from_last(low, 1), from_last(high, -1)
    after_low, before_high, lists = together(after_low, before_high, lists)
    after_high, before_low = from_last(high, 1), from_last(low, -1)
    after_high, before_low, lent = together(after_high, before_low, lent)
    buffers = [plane, after_low, after_high, from_last(after_low, 1), from_last(before_high, -1), before_low, before_high]
    buffers += [from_core(a) for a in buffers]
    back = from_borrower(multiply(1, lists, lent, buffers))
    here = multiply(0, lists, mine, buffers)
    aggregated = (here + back).astype(jnp.bfloat16)
    product = jnp.dot(aggregated, weight, preferred_element_type=jnp.float32)
    return jnp.maximum(product, 0.0).astype(jnp.bfloat16)


def solution(mesh):
    grid = Mesh(mesh.devices.reshape(DIMS), AXES)
    return jax.shard_map(
        on_device,
        mesh=grid,
        in_specs=(P(AXES, None), P(AXES, None, None, None), P(AXES, None), P()),
        out_specs=P(AXES, None),
        check_vma=False,
    )
```

```python
import itertools

import jax
import jax.numpy as jnp
from jax import lax
from jax.experimental import pallas as pl
from jax.experimental.pallas import tpu as pltpu
from jax.sharding import Mesh, PartitionSpec as P

AXES = ("yh", "zh", "zl", "x", "yl", "core")
DIMS = (2, 4, 2, 4, 2, 2)
SIDE = 128
WIDTH = 256
TILES = 64
PLANE = 16
BUFFERS = 7
BATCH = 12


def move(a, target):
    found = []
    for source, (yh, zh, zl, x, yl, core) in enumerate(itertools.product(*map(range, DIMS))):
        tx, ty, tz, tc = target(x, yh * 2 + yl, zh * 2 + zl, core)
        tx, ty, tz = tx % 4, ty % 4, tz % 8
        found.append((source, ((((ty // 2) * 8 + tz) * 4 + tx) * 2 + ty % 2) * 2 + tc))
    return lax.ppermute(a, AXES, found)


def from_line(a, d):
    return move(a, lambda x, y, z, c: (x, y, z - 2 * d, c))


def from_middle(a, d):
    return move(a, lambda x, y, z, c: (x, y - d, z, c) if c == 0 else (x - d, y, z, c))


def from_last(a, d):
    return move(a, lambda x, y, z, c: (x - d, y, z, c) if c == 0 else (x, y - d, z, c))


def from_core(a):
    return move(a, lambda x, y, z, c: (x, y, z, 1 - c))


def from_lender(a):
    return move(a, lambda x, y, z, c: (x, y, z + 1 - 2 * c, c))


def from_borrower(a):
    return move(a, lambda x, y, z, c: (x, y, z - 1 + 2 * c, c))


def places(columns):
    yh, zh, zl, x, yl, core = (lax.axis_index(a) for a in AXES)
    y = yh * 2 + yl
    at = columns & 1
    dz = (((columns >> 5) & 3) - zh) & 3
    dx = (((columns >> 2) & 3) - x) & 3
    dy = (((columns >> 7) * 2 + ((columns >> 1) & 1)) - y) & 3
    middle = jnp.where(at == 0, dy, dx)
    last = jnp.where(at == 0, dx, dy)
    inner = middle * 4 + dz
    buffer = jnp.where(last == 0, 0, last * 2 - 1 + (inner >> 3))
    place = ((at ^ core) * BUFFERS + buffer) * PLANE + inner
    return jnp.where(((columns >> 4) & 1) == zl, place, -1)


def list_kernel(place_ref, list_ref):
    for r in range(2):

        def step(k, counts):
            place = place_ref[r, k]
            held, far = place >= 0, place >= BUFFERS * PLANE
            list_ref[2 * r, counts[0]] = (k << 8) + (place & 255)
            list_ref[2 * r + 1, counts[1]] = (k << 8) + ((place - BUFFERS * PLANE) & 255)
            return jnp.where(held & ~far, counts[0] + 1, counts[0]), jnp.where(far, counts[1] + 1, counts[1])

        counts = lax.fori_loop(0, TILES, step, (0, 0))
        list_ref[2 * r, TILES] = counts[0]
        list_ref[2 * r + 1, TILES] = counts[1]


def listed(place):
    smem = pl.BlockSpec(memory_space=pltpu.SMEM)
    return pl.pallas_call(
        list_kernel,
        out_shape=jax.ShapeDtypeStruct((4, TILES + 1), jnp.int32),
        in_specs=[smem],
        out_specs=smem,
        compiler_params=pltpu.CompilerParams(vmem_limit_bytes=1024 * 1024),
    )(place)


def rows(index):
    return pl.ds(pl.multiple_of(index << 7, SIDE), SIDE)


def multiply(row, lists, tiles, buffers):
    vmem = pl.BlockSpec(memory_space=pltpu.VMEM)

    def kernel(list_ref, tiles_ref, *rest):
        out_ref = rest[-1]
        out_ref[...] = jnp.zeros_like(out_ref)
        for side in range(2):
            held = rest[side * BUFFERS : (side + 1) * BUFFERS]
            which = 2 * row + side
            n = list_ref[which, TILES]

            @pl.loop(0, (n + BATCH - 1) // BATCH)
            def _(i):
                left, right = [], []
                for j in range(BATCH):
                    at = i * BATCH + j
                    code = list_ref[which, jnp.minimum(at, n - 1)]
                    tile = tiles_ref[rows(code >> 8), :]
                    left.append(jnp.where(at < n, tile, jnp.zeros_like(tile)))
                    buffer = (code >> 4) & 15
                    block = held[0][rows(code & 15), :]
                    for b in range(1, BUFFERS):
                        block = jnp.where(buffer == b, held[b][rows(code & 7), :], block)
                    right.append(block)
                out_ref[...] += jnp.dot(
                    jnp.concatenate(left, axis=1), jnp.concatenate(right, axis=0), preferred_element_type=jnp.float32
                )

    held = [pltpu.with_memory_space_constraint(a, pltpu.VMEM) for a in (tiles, *buffers)]
    return pl.pallas_call(
        kernel,
        out_shape=jax.ShapeDtypeStruct((SIDE, WIDTH), jnp.float32),
        in_specs=[pl.BlockSpec(memory_space=pltpu.SMEM)] + [vmem] * len(held),
        out_specs=vmem,
        compiler_params=pltpu.CompilerParams(vmem_limit_bytes=16 * 1024 * 1024),
        cost_estimate=pl.CostEstimate(flops=32 * 2 * SIDE * SIDE * WIDTH, bytes_accessed=3 << 20, transcendentals=0),
    )(lists, *held)


def together(*arrays):
    return lax.optimization_barrier(arrays)


def on_device(features, tiles, columns, weight):
    mine = tiles.reshape(TILES * SIDE, SIDE)
    place = places(jnp.concatenate([columns, from_lender(columns)], axis=0))
    lines = [features] + [from_line(features, d) for d in (1, 2, 3)]
    line = jnp.concatenate(lines, axis=0)
    line, place, sent = together(line, place, mine)
    lent = from_lender(sent)
    plane = jnp.concatenate([line] + [from_middle(line, d) for d in (1, 2, 3)], axis=0)
    plane, lists = together(plane, listed(place))
    half = PLANE // 2 * SIDE
    low, high = plane[:half], plane[half:]
    after_low, before_high = from_last(low, 1), from_last(high, -1)
    after_low, before_high = together(after_low, before_high)
    after_high, before_low = from_last(high, 1), from_last(low, -1)
    after_high, before_low, lent = together(after_high, before_low, lent)
    buffers = [plane, after_low, after_high, from_last(after_low, 1), from_last(before_high, -1), before_low, before_high]
    buffers += [from_core(a) for a in buffers]
    back = from_borrower(multiply(1, lists, lent, buffers))
    here = multiply(0, lists, mine, buffers)
    aggregated = (here + back).astype(jnp.bfloat16)
    product = jnp.dot(aggregated, weight, preferred_element_type=jnp.float32)
    return jnp.maximum(product, 0.0).astype(jnp.bfloat16)


def solution(mesh):
    grid = Mesh(mesh.devices.reshape(DIMS), AXES)
    return jax.shard_map(
        on_device,
        mesh=grid,
        in_specs=(P(AXES, None), P(AXES, None, None, None), P(AXES, None), P()),
        out_specs=P(AXES, None),
        check_vma=False,
    )
```
